256 devices in a mesh: row: 128 (over z_lo, x, y, core), col: 2 (over z_hi).
Axes of the slice: x: 4, y: 4, z: 8 (z_hi: 2, z_lo: 4; z = z_hi * 4 + z_lo), core: 2. Of those that a mesh axis runs over, the one named last changes fastest.
Arguments:
- snapshot: float32 [4, 262144, 512], P(None, 'row', 'col'), may hold values from -6 to 6
- range_test: float32 [4, 129, 512], P(None, None, 'col'), may hold values from -0.125 to 0.125
- corange_test: float32 [129, 262144], P(None, 'row'), may hold values from -0.01171875 to 0.01171875
- core_left: float32 [259, 262144], P(None, 'row'), may hold values from -0.01171875 to 0.01171875
- core_right: float32 [4, 259, 512], P(None, None, 'col'), may hold values from -0.125 to 0.125
- range_sketch: float32 [129, 262144], P(None, ('row', 'col')), may hold values from -6 to 6
- core_sketch: float32 [259, 259], replicated, may hold values from -6 to 6
Outputs:
- range_out: float32 [129, 262144], P(None, ('row', 'col'))
- corange_out: float32 [4, 129, 512], P(None, None, 'col')
- core_out: float32 [259, 259], replicated
The draws below stay inside these ranges and needn't reach their ends.
All inputs are finite; a program needn't handle non-finite values.
Results may differ from the reference program's by a relative error of at most 0.0001.
Values sent between devices are 32-bit elements; how exact they have to be, the bound alone decides.
No kernel may reach another device: no remote copies, remote signals or barrier semaphores. Data moves between devices by JAX's collectives and lax.ppermute only.
A program may use at most 64 MiB of HBM per device.

```python
import jax
import jax.numpy as jnp
from jax import lax

K = 129
S = 259
COLS = 512
SLABS = 4
M = 262144


def shard_levels(rng, dims, split, least, top_value):
    def one(position, blocks):
        draws = jax.random.uniform(jax.random.fold_in(jax.random.fold_in(rng, 6), position), (blocks,), jnp.float32, least / len(split), top_value / len(split))
        return jnp.repeat(jnp.exp(draws), dims[position] // blocks).reshape((-1,) + (1,) * (len(dims) - position - 1))

    factor_of = one(*split[0])
    for cut in split[1:]:
        factor_of = factor_of * one(*cut)
    return factor_of


def normal_values(own_key, shape, spread, bound, shards=(), dtype=jnp.bfloat16):
    values = jax.random.normal(own_key, shape, jnp.float32) * spread
    if len(shards) > 0:
        values = shard_levels(own_key, shape, shards, -0.22, 0.18) * values
    return jnp.clip(values, min=-bound, max=bound).astype(dtype)


def setup_inputs(seed: int = 0) -> dict:
    arg_keys = jax.random.split(jax.random.key(seed), 8)
    return {
        "snapshot": normal_values(arg_keys[0], (SLABS, M, COLS), 1.0, 6.0, ((1, 128), (2, 2)), jnp.float32),
        "range_test": normal_values(arg_keys[1], (SLABS, K, COLS), (SLABS * COLS) ** -0.5, 0.125, ((2, 2),), jnp.float32),
        "corange_test": normal_values(arg_keys[2], (K, M), M ** -0.5, 0.01171875, ((1, 128),), jnp.float32),
        "core_left": normal_values(arg_keys[3], (S, M), M ** -0.5, 0.01171875, ((1, 128),), jnp.float32),
        "core_right": normal_values(arg_keys[4], (SLABS, S, COLS), (SLABS * COLS) ** -0.5, 0.125, ((2, 2),), jnp.float32),
        "range_sketch": normal_values(arg_keys[5], (K, M), 1.0, 6.0, ((1, 256),), jnp.float32),
        "core_sketch": normal_values(arg_keys[6], (S, S), 1.0, 6.0, (), jnp.float32),
    }


def reference(snapshot, range_test, corange_test, core_left, core_right, range_sketch, core_sketch):
    highest = lax.Precision.HIGHEST

    def absorb(totals, pieces):
        range_acc, core_acc = totals
        slab_block, range_block, right_block = pieces
        range_acc = range_acc + jnp.dot(range_block, slab_block.T, precision=highest, preferred_element_type=jnp.float32)
        corange = jnp.dot(corange_test, slab_block, precision=highest, preferred_element_type=jnp.float32)
        left_prod = jnp.dot(core_left, slab_block, precision=highest, preferred_element_type=jnp.float32)
        core_acc = core_acc + jnp.dot(left_prod, right_block.T, precision=highest, preferred_element_type=jnp.float32)
        return (range_acc, core_acc), corange

    (range_out, core_out), corange_out = lax.scan(absorb, (range_sketch, core_sketch), (snapshot, range_test, core_right))
    return range_out, corange_out, core_out
```

```python
import jax
import jax.numpy as jnp
from jax import lax
from jax.experimental import pallas as pl
from jax.experimental.pallas import tpu as pltpu
from jax.sharding import Mesh
from jax.sharding import PartitionSpec as P

ROWS = 896
CORE_AT = 544
EXTRA_AT = 808
CHUNK = 56
BLOCK = 256


def split(x):
    high = x.astype(jnp.bfloat16)
    low = (x - high.astype(jnp.float32)).astype(jnp.bfloat16)
    return high, low


def products(
    place, snap_ref, range_test_ref, corange_ref, left_ref, right_ref, sketch_ref,
    send_ref, keep_ref, mine_ref, other_ref,
    test_cat, corange_acc, left_acc,
):
    step = pl.program_id(0)
    steps = pl.num_programs(0)
    slabs, _, cols = snap_ref.shape

    @pl.when(step == 0)
    def _():
        for j in range(slabs):
            high, low = split(range_test_ref[j])
            at = 3 * cols * j
            test_cat[:, at : at + cols] = high
            test_cat[:, at + cols : at + 2 * cols] = high
            test_cat[:, at + 2 * cols : at + 3 * cols] = low
        corange_acc[...] = jnp.zeros_like(corange_acc)
        left_acc[...] = jnp.zeros_like(left_acc)

    high, low = split(corange_ref[...])
    corange_cat = jnp.concatenate([high, high, low], axis=1)
    high, low = split(left_ref[...])
    left_cat = jnp.concatenate([high, high, low], axis=1)
    pieces = []
    for j in range(slabs):
        high, low = split(snap_ref[j])
        pieces += [high, low, high]
        snap_cat = jnp.concatenate([high, low, high], axis=0)
        corange_acc[j] += jnp.dot(corange_cat, snap_cat, preferred_element_type=jnp.float32)
        left_acc[j] += jnp.dot(left_cat, snap_cat, preferred_element_type=jnp.float32)
    range_part = lax.dot_general(
        test_cat[...], jnp.concatenate(pieces, axis=1), (((1,), (1,)), ((), ())),
        preferred_element_type=jnp.float32,
    )

    @pl.when(step < steps // 2)
    def _():
        send_ref[...] = range_part

    @pl.when(step >= steps // 2)
    def _():
        keep_ref[...] = sketch_ref[...] + range_part

    @pl.when(step == steps - 1)
    def _():
        size = right_ref.shape[1]
        lefts, rights = [], []
        for j in range(slabs):
            high, low = split(left_acc[j])
            lefts += [high, high, low]
            high, low = split(right_ref[j])
            rights += [high, low, high]
        left_all = jnp.concatenate(lefts, axis=1)
        right_all = jnp.concatenate(rights, axis=1)
        core = lax.dot_general(
            left_all, right_all[:256], (((1,), (1,)), ((), ())), preferred_element_type=jnp.float32
        )
        extra = lax.dot_general(
            right_all[256:], left_all, (((1,), (1,)), ((), ())), preferred_element_type=jnp.float32
        )
        more = size - 256
        for own in range(2):

            @pl.when(place[1] == own)
            def _():
                for half, out in ((own, mine_ref), (1 - own, other_ref)):
                    lanes = slice(128 * half, 128 * half + 128)
                    out[...] = jnp.zeros_like(out)
                    for j in range(slabs):
                        out[136 * j : 136 * j + corange_ref.shape[0], :] = corange_acc[j, :, lanes]
                    out[CORE_AT : CORE_AT + size, :] = core[:, lanes]
                    out[EXTRA_AT : EXTRA_AT + more, :] = extra[:, lanes]
                    if half == 0:
                        out[EXTRA_AT + 8 : EXTRA_AT + 8 + more, :more] = extra[:, 256:]


def finish(place, mine_ref, other_ref, core_sketch_ref, keep_ref, got_ref, range_ref, corange_ref, core_ref):
    range_ref[...] = keep_ref[...] + got_ref[...]
    slabs, rank, _ = corange_ref.shape
    size = core_ref.shape[0]
    more = size - 256
    for own in range(2):

        @pl.when(place[1] == own)
        def _():
            for half, part in ((own, mine_ref), (1 - own, other_ref)):
                lanes = slice(128 * half, 128 * half + 128)
                for j in range(slabs):
                    corange_ref[j, :, lanes] = part[136 * j : 136 * j + rank, :]
                core_ref[:, lanes] = core_sketch_ref[:, lanes] + part[CORE_AT : CORE_AT + size, :]
                block = jnp.concatenate([part[EXTRA_AT : EXTRA_AT + 8, :], jnp.zeros((120, 128), jnp.float32)], axis=0)
                turned = block.T
                core_ref[lanes, 256:] = core_sketch_ref[lanes, 256:] + turned[:, :more]
                if half == 0:
                    block = jnp.concatenate(
                        [part[EXTRA_AT + 8 : EXTRA_AT + 16, :], jnp.zeros((120, 128), jnp.float32)], axis=0
                    )
                    turned = block.T
                    core_ref[256:, 256:] = core_sketch_ref[256:, 256:] + turned[:more, :more]


def on_device(snapshot, range_test, corange_test, core_left, core_right, range_sketch, core_sketch):
    slabs, rows, cols = snapshot.shape
    rank = range_test.shape[1]
    size = core_left.shape[0]
    width = rows // 2
    steps = rows // BLOCK
    half = steps // 2
    column = lax.axis_index("zh")
    core = lax.axis_index("core")
    place = jnp.stack([column, core]).astype(jnp.int32)

    def turn(i, p):
        return lax.rem(i + half * (1 - p[0]), steps)

    vmem = pl.BlockSpec(memory_space=pltpu.VMEM)
    send, keep, mine, other = pl.pallas_call(
        products,
        out_shape=(
            jax.ShapeDtypeStruct((rank, width), jnp.float32),
            jax.ShapeDtypeStruct((rank, width), jnp.float32),
            jax.ShapeDtypeStruct((ROWS, 128), jnp.float32),
            jax.ShapeDtypeStruct((ROWS, 128), jnp.float32),
        ),
        grid_spec=pltpu.PrefetchScalarGridSpec(
            num_scalar_prefetch=1,
            grid=(steps,),
            in_specs=[
                pl.BlockSpec((slabs, BLOCK, cols), lambda i, p: (0, turn(i, p), 0)),
                pl.BlockSpec((slabs, rank, cols), lambda i, p: (0, 0, 0)),
                pl.BlockSpec((rank, BLOCK), lambda i, p: (0, turn(i, p))),
                pl.BlockSpec((size, BLOCK), lambda i, p: (0, turn(i, p))),
                pl.BlockSpec((slabs, size, cols), lambda i, p: (0, 0, 0)),
                pl.BlockSpec((rank, BLOCK), lambda i, p: (0, jnp.maximum(i - half, 0))),
            ],
            out_specs=[
                pl.BlockSpec((rank, BLOCK), lambda i, p: (0, jnp.minimum(i, half - 1))),
                pl.BlockSpec((rank, BLOCK), lambda i, p: (0, jnp.maximum(i - half, 0))),
                pl.BlockSpec((ROWS, 128), lambda i, p: (0, 0)),
                pl.BlockSpec((ROWS, 128), lambda i, p: (0, 0)),
            ],
            scratch_shapes=[
                pltpu.VMEM((rank, 3 * cols * slabs), jnp.bfloat16),
                pltpu.VMEM((slabs, rank, cols), jnp.float32),
                pltpu.VMEM((slabs, size, cols), jnp.float32),
            ],
        ),
        compiler_params=pltpu.CompilerParams(vmem_limit_bytes=40 * 2**20),
        cost_estimate=pl.CostEstimate(flops=7_000_000_000, bytes_accessed=15_000_000, transcendentals=0),
        name="products",
    )(place, snapshot, range_test, corange_test, core_left, core_right, range_sketch)

    got = lax.ppermute(send, "zh", [(0, 1), (1, 0)])
    swap = [(0, 1), (1, 0)]
    part = mine + lax.ppermute(other, "core", swap)
    pieces = lax.all_to_all(part.reshape(16, CHUNK, 128), ("x", "y"), 0, 0, tiled=True)
    piece = pieces.sum(axis=0)
    stack = lax.all_to_all(jnp.broadcast_to(piece[None], (8, CHUNK, 128)), ("zh", "zl"), 0, 0, tiled=True)
    at = CHUNK * lax.axis_index(("x", "y")) + lax.broadcasted_iota(jnp.int32, (CHUNK, 128), 0)
    both = stack.reshape(2, 4, CHUNK, 128).sum(axis=1)
    total = jnp.where(at >= CORE_AT, both[0] + both[1], jnp.where(column == 0, both[0], both[1]))
    mine = lax.all_to_all(jnp.broadcast_to(total[None], (16, CHUNK, 128)), ("x", "y"), 0, 0, tiled=True)
    mine = mine.reshape(ROWS, 128)
    other = lax.ppermute(mine, "core", swap)

    return pl.pallas_call(
        finish,
        out_shape=(
            jax.ShapeDtypeStruct((rank, width), jnp.float32),
            jax.ShapeDtypeStruct((slabs, rank, cols), jnp.float32),
            jax.ShapeDtypeStruct((size, size), jnp.float32),
        ),
        in_specs=[pl.BlockSpec(memory_space=pltpu.SMEM)] + [vmem] * 5,
        out_specs=[vmem] * 3,
        compiler_params=pltpu.CompilerParams(vmem_limit_bytes=40 * 2**20),
        name="finish",
    )(place, mine, other, core_sketch, keep, got)


def solution(mesh):
    fine = Mesh(mesh.devices.reshape(4, 4, 4, 2, 2), ("zl", "x", "y", "core", "zh"))
    row = ("zl", "x", "y", "core")
    placed = (
        P(None, row, "zh"),
        P(None, None, "zh"),
        P(None, row),
        P(None, row),
        P(None, None, "zh"),
        P(None, row + ("zh",)),
        P(),
    )
    return jax.shard_map(
        on_device,
        mesh=fine,
        in_specs=placed,
        out_specs=(P(None, row + ("zh",)), P(None, None, "zh"), P()),
        check_vma=False,
    )
```

```python
import jax
import jax.numpy as jnp
from jax import lax
from jax.experimental import pallas as pl
from jax.experimental.pallas import tpu as pltpu
from jax.sharding import Mesh
from jax.sharding import PartitionSpec as P

ROWS = 896
CORE_AT = 544
EXTRA_AT = 808
CHUNK = 56
SLAB = 136
LEFT_AT = 144
PIECE = 512
SPANS = ((0, 1024),)


def split(x):
    high = x.astype(jnp.bfloat16)
    low = (x - high.astype(jnp.float32)).astype(jnp.bfloat16)
    return high, low


NT = (((1,), (1,)), ((), ()))


def reductions(place, snap_ref, corange_ref, left_ref, right_hbm, mine_ref, other_ref, tests, acc, pay, core_acc, extra_acc, right, sem):
    slab = pl.program_id(0)
    rank = corange_ref.shape[0]
    size = left_ref.shape[0]
    more = size - 256

    @pl.when(slab == 0)
    def _():
        for j in range(right.shape[0]):
            pltpu.make_async_copy(right_hbm.at[:, j, :], right.at[j], sem.at[j]).start()
        high, low = split(corange_ref[...])
        tests[:rank] = jnp.concatenate([high, high, low], axis=1)
        high, low = split(left_ref[...])
        tests[LEFT_AT:] = jnp.concatenate([high, high, low], axis=1)
        core_acc[...] = jnp.zeros_like(core_acc)
        extra_acc[...] = jnp.zeros_like(extra_acc)

    high, low = split(snap_ref[0])
    acc[...] = jnp.dot(tests[...], jnp.concatenate([high, low, high], axis=0), preferred_element_type=jnp.float32)
    for half in range(2):
        pay[place[1] ^ half, pl.ds(pl.multiple_of(SLAB * slab, 8), SLAB), :] = acc[:SLAB, 128 * half : 128 * half + 128]
    high, low = split(acc[LEFT_AT:])
    left = jnp.concatenate([high, high, low], axis=1)
    pltpu.make_async_copy(right_hbm.at[:, 0, :], right.at[slab], sem.at[slab]).wait()
    high, low = split(right[slab])
    turned = jnp.concatenate([high, low, high], axis=1)
    core_acc[:size] += lax.dot_general(left, turned[:256], NT, preferred_element_type=jnp.float32)
    extra_acc[:more] += lax.dot_general(turned[256:], left, NT, preferred_element_type=jnp.float32)

    @pl.when(slab == pl.num_programs(0) - 1)
    def _():
        for half in range(2):
            lanes = slice(128 * half, 128 * half + 128)
            own = place[1] ^ half
            pay[own, CORE_AT : CORE_AT + size, :] = core_acc[:size, lanes]
            pay[own, EXTRA_AT : EXTRA_AT + 8, :] = extra_acc[:, lanes]
        pay[place[1], EXTRA_AT + 8 : EXTRA_AT + 16, :more] = extra_acc[:, 256:]
        mine_ref[...] = pay[0]
        other_ref[...] = pay[1]


def range_half(place, snap_hbm, test_hbm, *rest):
    *extra, out_ref, snap, test, test_sem, sem = rest
    kept = extra[0] if len(extra) and extra[0].shape[0] == out_ref.shape[0] and len(extra) == 2 else None
    slabs, width, _ = snap.shape
    count = width // PIECE
    at = place[0] * width
    loads = [pltpu.make_async_copy(test_hbm.at[:, j, :], test.at[j], test_sem.at[j]) for j in range(slabs)]
    for copy in loads:
        copy.start()
    copies = []
    for c in range(count):
        copy = pltpu.make_async_copy(
            snap_hbm.at[:, pl.ds(pl.multiple_of(at + c * PIECE, PIECE), PIECE), :],
            snap.at[:, pl.ds(c * PIECE, PIECE), :],
            sem.at[c],
        )
        copy.start()
        copies.append(copy)
    tests = []
    for j in range(slabs):
        loads[j].wait()
        high, low = split(test[j])
        tests += [high, high, low]
    tests = jnp.concatenate(tests, axis=1)
    for c in range(count):
        copies[c].wait()
        pieces = []
        for j in range(slabs):
            high, low = split(snap[j, c * PIECE : (c + 1) * PIECE, :])
            pieces += [high, low, high]
        cols = slice(c * PIECE, (c + 1) * PIECE)
        part = lax.dot_general(tests, jnp.concatenate(pieces, axis=1), NT, preferred_element_type=jnp.float32)
        out_ref[:, cols] = part if kept is None else kept[:, cols] + part


def add_two(a_ref, b_ref, *rest):
    rest[-1][...] = a_ref[...] + b_ref[...]


def sum_pieces(pieces_ref, *rest):
    out_ref = rest[-1]
    total = pieces_ref[0]
    for k in range(1, pieces_ref.shape[0]):
        total += pieces_ref[k]
    for k in range(out_ref.shape[0]):
        out_ref[k] = total


def sum_stack(place, stack_ref, *rest):
    out_ref = rest[-1]
    near = stack_ref[4 * place[0]]
    far = stack_ref[4 - 4 * place[0]]
    for k in range(1, 4):
        near += stack_ref[4 * place[0] + k]
        far += stack_ref[4 - 4 * place[0] + k]
    at = CHUNK * place[2] + lax.broadcasted_iota(jnp.int32, near.shape, 0)
    total = jnp.where(at >= CORE_AT, near + far, near)
    for k in range(out_ref.shape[0]):
        out_ref[k] = total


def finish(place, mine_ref, other_ref, core_sketch_ref, keep_ref, *rest):
    *got_refs, range_ref, corange_ref, core_ref = rest
    at = 0
    for got in got_refs:
        cols = slice(at, at + got.shape[1])
        range_ref[:, cols] = keep_ref[:, cols] + got[...]
        at += got.shape[1]
    rank, slabs, _ = corange_ref.shape
    size = core_ref.shape[0]
    more = size - 256
    for own in range(2):

        @pl.when(place[1] == own)
        def _():
            for half, part in ((own, mine_ref), (1 - own, other_ref)):
                lanes = slice(128 * half, 128 * half + 128)
                for j in range(slabs):
                    corange_ref[:, j, lanes] = part[SLAB * j : SLAB * j + rank, :]
                core_ref[:, lanes] = core_sketch_ref[:, lanes] + part[CORE_AT : CORE_AT + size, :]
                block = jnp.concatenate([part[EXTRA_AT : EXTRA_AT + 8, :], jnp.zeros((120, 128), jnp.float32)], axis=0)
                turned = block.T
                core_ref[lanes, 256:] = core_sketch_ref[lanes, 256:] + turned[:, :more]
                if half == 0:
                    block = jnp.concatenate(
                        [part[EXTRA_AT + 8 : EXTRA_AT + 16, :], jnp.zeros((120, 128), jnp.float32)], axis=0
                    )
                    turned = block.T
                    core_ref[256:, 256:] = core_sketch_ref[256:, 256:] + turned[:more, :more]


def on_device(snapshot, range_test, corange_test, core_left, core_right, range_sketch, core_sketch):
    slabs, rows, cols = snapshot.shape
    rank = range_test.shape[1]
    size = core_left.shape[0]
    width = rows // 2
    column = lax.axis_index("zh")
    place = jnp.stack([column, lax.axis_index("core"), lax.axis_index(("x", "y"))]).astype(jnp.int32)
    flip = jnp.stack([1 - column]).astype(jnp.int32)
    vmem = pl.BlockSpec(memory_space=pltpu.VMEM)
    smem = pl.BlockSpec(memory_space=pltpu.SMEM)
    anywhere = pl.BlockSpec(memory_space=pl.ANY)
    params = pltpu.CompilerParams(vmem_limit_bytes=16 * 2**20)
    f32 = lambda *shape: jax.ShapeDtypeStruct(shape, jnp.float32)

    def cost(us):
        return pl.CostEstimate(flops=int(us * 1e9), bytes_accessed=int(us * 3e6), transcendentals=0)

    mine, other = pl.pallas_call(
        reductions,
        out_shape=(f32(ROWS, 128), f32(ROWS, 128)),
        grid_spec=pltpu.PrefetchScalarGridSpec(
            num_scalar_prefetch=1,
            grid=(slabs,),
            in_specs=[
                pl.BlockSpec((1, rows, cols), lambda i, p: (i, 0, 0)),
                pl.BlockSpec((rank, rows), lambda i, p: (0, 0)),
                pl.BlockSpec((size, rows), lambda i, p: (0, 0)),
                anywhere,
            ],
            out_specs=[pl.BlockSpec((ROWS, 128), lambda i, p: (0, 0))] * 2,
            scratch_shapes=[
                pltpu.VMEM((LEFT_AT + size, 3 * rows), jnp.bfloat16),
                pltpu.VMEM((LEFT_AT + size, cols), jnp.float32),
                pltpu.VMEM((2, ROWS, 128), jnp.float32),
                pltpu.VMEM((264, 256), jnp.float32),
                pltpu.VMEM((8, size), jnp.float32),
                pltpu.VMEM((slabs, size, cols), jnp.float32),
                pltpu.SemaphoreType.DMA((slabs,)),
            ],
        ),
        compiler_params=pltpu.CompilerParams(vmem_limit_bytes=60 * 2**20),
        cost_estimate=cost(9),
        name="reductions",
    )(place, snapshot, corange_test, core_left, jnp.transpose(core_right, (1, 0, 2)))

    def range_part(name, where, kept, *more):
        return pl.pallas_call(
            range_half,
            out_shape=f32(rank, width),
            in_specs=[smem, anywhere, anywhere] + [vmem] * kept + [anywhere] * (len(more) - kept),
            out_specs=vmem,
            scratch_shapes=[
                pltpu.VMEM((slabs, width, cols), jnp.float32),
                pltpu.VMEM((slabs, rank, cols), jnp.float32),
                pltpu.SemaphoreType.DMA((slabs,)),
                pltpu.SemaphoreType.DMA((width // PIECE,)),
            ],
            compiler_params=pltpu.CompilerParams(vmem_limit_bytes=54 * 2**20),
            cost_estimate=cost(5),
            name=name,
        )(where, snapshot, jnp.transpose(range_test, (1, 0, 2)), *more)

    def add_up(kernel, name, shape, *args):
        specs = [smem] * (kernel is sum_stack) + [vmem] * (1 + (kernel is add_two))
        specs += [anywhere] * (len(args) - len(specs))
        return pl.pallas_call(
            kernel,
            out_shape=f32(*shape),
            in_specs=specs,
            out_specs=vmem,
            compiler_params=params,
            cost_estimate=cost(1),
            name=name,
        )(*args)

    swap = [(0, 1), (1, 0)]
    send = range_part("range_send", flip, 0, mine)
    part = add_up(add_two, "add_two", (ROWS, 128), mine, lax.ppermute(other, "core", swap), send)
    got = [lax.ppermute(send[:, a:b], "zh", swap) for a, b in SPANS] if len(SPANS) > 1 else [lax.ppermute(send, "zh", swap)]

    def reduce(part):
        pieces = lax.all_to_all(part.reshape(16, CHUNK, 128), ("x", "y"), 0, 0, tiled=True)
        keep = range_part("range_keep", place, 1, range_sketch, part)
        copies = add_up(sum_pieces, "sum_pieces", (8, CHUNK, 128), pieces, keep)
        stack = lax.all_to_all(copies, ("zh", "zl"), 0, 0, tiled=True)
        copies = add_up(sum_stack, "sum_stack", (16, CHUNK, 128), place, stack)
        mine = lax.all_to_all(copies, ("x", "y"), 0, 0, tiled=True).reshape(ROWS, 128)
        return mine, keep

    def nothing(part):
        return jnp.zeros((ROWS, 128), jnp.float32), jnp.zeros((rank, width), jnp.float32)

    mine, keep = lax.cond(place[0] >= 0, reduce, nothing, part)
    other = lax.ppermute(mine, "core", swap)

    range_out, corange_out, core_out = pl.pallas_call(
        finish,
        out_shape=(f32(rank, width), f32(rank, slabs, cols), f32(size, size)),
        in_specs=[smem] + [vmem] * (4 + len(got)),
        out_specs=[vmem] * 3,
        compiler_params=params,
        cost_estimate=cost(2),
        name="finish",
    )(place, mine, other, core_sketch, keep, *got)
    return range_out, jnp.transpose(corange_out, (1, 0, 2)), core_out


def solution(mesh):
    fine = Mesh(mesh.devices.reshape(4, 4, 4, 2, 2), ("zl", "x", "y", "core", "zh"))
    row = ("zl", "x", "y", "core")
    placed = (
        P(None, row, "zh"),
        P(None, None, "zh"),
        P(None, row),
        P(None, row),
        P(None, None, "zh"),
        P(None, row + ("zh",)),
        P(),
    )
    return jax.shard_map(
        on_device,
        mesh=fine,
        in_specs=placed,
        out_specs=(P(None, row + ("zh",)), P(None, None, "zh"), P()),
        check_vma=False,
    )
```

```python
import jax
import jax.numpy as jnp
from jax import lax
from jax.experimental import pallas as pl
from jax.experimental.pallas import tpu as pltpu
from jax.sharding import Mesh
from jax.sharding import PartitionSpec as P

ROWS = 896
CORE_AT = 544
EXTRA_AT = 808
CHUNK = 56
SLAB = 136
LEFT_AT = 144
PIECE = 512
BLOCK = 512


def split(x):
    high = x.astype(jnp.bfloat16)
    low = (x - high.astype(jnp.float32)).astype(jnp.bfloat16)
    return high, low


NT = (((1,), (1,)), ((), ()))


def products(
    place, snap_ref, corange_ref, left_ref, right_hbm, after,
    mine_ref, other_ref,
    tests, acc, pay, core_acc, extra_acc, right, sem,
):
    step = pl.program_id(0)
    steps = pl.num_programs(0)
    slabs, _, cols = snap_ref.shape
    rank = corange_ref.shape[0]
    size = left_ref.shape[0]
    more = size - 256
    loads = [pltpu.make_async_copy(right_hbm.at[:, j, :], right.at[j], sem.at[j]) for j in range(slabs)]

    @pl.when(step == 0)
    def _():
        for copy in loads:
            copy.start()
        acc[...] = jnp.zeros_like(acc)
        tests[rank:LEFT_AT] = jnp.zeros((LEFT_AT - rank, tests.shape[1]), jnp.bfloat16)

    high, low = split(corange_ref[...])
    tests[:rank] = jnp.concatenate([high, high, low], axis=1)
    high, low = split(left_ref[...])
    tests[LEFT_AT:] = jnp.concatenate([high, high, low], axis=1)
    for j in range(slabs):
        high, low = split(snap_ref[j])
        acc[j] += jnp.dot(
            tests[...], jnp.concatenate([high, low, high], axis=0), preferred_element_type=jnp.float32
        )

    @pl.when(step == steps - 1)
    def _():
        lefts, rights = [], []
        for j in range(slabs):
            for half in range(2):
                pay[place[1] ^ half, SLAB * j : SLAB * (j + 1), :] = acc[j, :SLAB, 128 * half : 128 * half + 128]
            loads[j].wait()
            high, low = split(acc[j, LEFT_AT:])
            lefts += [high, high, low]
            high, low = split(right[j])
            rights += [high, low, high]
        left_all = jnp.concatenate(lefts, axis=1)
        right_all = jnp.concatenate(rights, axis=1)
        core_acc[:size] = lax.dot_general(left_all, right_all[:256], NT, preferred_element_type=jnp.float32)
        extra_acc[:more] = lax.dot_general(right_all[256:], left_all, NT, preferred_element_type=jnp.float32)
        for half in range(2):
            lanes = slice(128 * half, 128 * half + 128)
            own = place[1] ^ half
            pay[own, CORE_AT : CORE_AT + size, :] = core_acc[:size, lanes]
            pay[own, EXTRA_AT : EXTRA_AT + more, :] = extra_acc[:more, lanes]
        pay[place[1], EXTRA_AT + 8 : EXTRA_AT + 8 + more, :more] = extra_acc[:more, 256:]
        mine_ref[...] = pay[0]
        other_ref[...] = pay[1]


def range_half(place, snap_hbm, test_hbm, *rest):
    *extra, out_ref, snap, test, test_sem, sem = rest
    kept = extra[0] if len(extra) and extra[0].shape[0] == out_ref.shape[0] and len(extra) == 2 else None
    slabs, width, _ = snap.shape
    count = width // PIECE
    at = place[0] * width
    loads = [pltpu.make_async_copy(test_hbm.at[:, j, :], test.at[j], test_sem.at[j]) for j in range(slabs)]
    for copy in loads:
        copy.start()
    copies = []
    for c in range(count):
        copy = pltpu.make_async_copy(
            snap_hbm.at[:, pl.ds(pl.multiple_of(at + c * PIECE, PIECE), PIECE), :],
            snap.at[:, pl.ds(c * PIECE, PIECE), :],
            sem.at[c],
        )
        copy.start()
        copies.append(copy)
    tests = []
    for j in range(slabs):
        loads[j].wait()
        high, low = split(test[j])
        tests += [high, high, low]
    tests = jnp.concatenate(tests, axis=1)
    for c in range(count):
        copies[c].wait()
        pieces = []
        for j in range(slabs):
            high, low = split(snap[j, c * PIECE : (c + 1) * PIECE, :])
            pieces += [high, low, high]
        cols = slice(c * PIECE, (c + 1) * PIECE)
        part = lax.dot_general(tests, jnp.concatenate(pieces, axis=1), NT, preferred_element_type=jnp.float32)
        out_ref[:, cols] = part if kept is None else kept[:, cols] + part


def sum_pieces(pieces_ref, *rest):
    out_ref = rest[-1]
    total = pieces_ref[0]
    for k in range(1, pieces_ref.shape[0]):
        total += pieces_ref[k]
    for k in range(out_ref.shape[0]):
        out_ref[k] = total


def sum_stack(place, stack_ref, *rest):
    out_ref = rest[-1]
    near = stack_ref[4 * place[0]]
    far = stack_ref[4 - 4 * place[0]]
    for k in range(1, 4):
        near += stack_ref[4 * place[0] + k]
        far += stack_ref[4 - 4 * place[0] + k]
    at = CHUNK * place[2] + lax.broadcasted_iota(jnp.int32, near.shape, 0)
    total = jnp.where(at >= CORE_AT, near + far, near)
    for k in range(out_ref.shape[0]):
        out_ref[k] = total


def finish(place, mine_ref, other_ref, core_sketch_ref, corange_ref, core_ref):
    rank, slabs, _ = corange_ref.shape
    size = core_ref.shape[0]
    more = size - 256
    for own in range(2):

        @pl.when(place[1] == own)
        def _():
            for half, part in ((own, mine_ref), (1 - own, other_ref)):
                lanes = slice(128 * half, 128 * half + 128)
                for j in range(slabs):
                    corange_ref[:, j, lanes] = part[SLAB * j : SLAB * j + rank, :]
                core_ref[:, lanes] = core_sketch_ref[:, lanes] + part[CORE_AT : CORE_AT + size, :]
                block = jnp.concatenate([part[EXTRA_AT : EXTRA_AT + 8, :], jnp.zeros((120, 128), jnp.float32)], axis=0)
                turned = block.T
                core_ref[lanes, 256:] = core_sketch_ref[lanes, 256:] + turned[:, :more]
                if half == 0:
                    block = jnp.concatenate(
                        [part[EXTRA_AT + 8 : EXTRA_AT + 16, :], jnp.zeros((120, 128), jnp.float32)], axis=0
                    )
                    turned = block.T
                    core_ref[256:, 256:] = core_sketch_ref[256:, 256:] + turned[:more, :more]


def on_device(snapshot, range_test, corange_test, core_left, core_right, range_sketch, core_sketch):
    slabs, rows, cols = snapshot.shape
    rank = range_test.shape[1]
    size = core_left.shape[0]
    width = rows // 2
    column = lax.axis_index("zh")
    place = jnp.stack([column, lax.axis_index("core"), lax.axis_index(("x", "y"))]).astype(jnp.int32)
    flip = jnp.stack([1 - column]).astype(jnp.int32)
    vmem = pl.BlockSpec(memory_space=pltpu.VMEM)
    smem = pl.BlockSpec(memory_space=pltpu.SMEM)
    anywhere = pl.BlockSpec(memory_space=pl.ANY)
    params = pltpu.CompilerParams(vmem_limit_bytes=16 * 2**20)
    f32 = lambda *shape: jax.ShapeDtypeStruct(shape, jnp.float32)

    def cost(us):
        return pl.CostEstimate(flops=int(us * 1e9), bytes_accessed=int(us * 3e6), transcendentals=0)

    tests_first = jnp.transpose(range_test, (1, 0, 2))
    def range_part(name, where, kept, *more):
        return pl.pallas_call(
            range_half,
            out_shape=f32(rank, width),
            in_specs=[smem, anywhere, anywhere] + [vmem] * kept + [anywhere] * (len(more) - kept),
            out_specs=vmem,
            scratch_shapes=[
                pltpu.VMEM((slabs, width, cols), jnp.float32),
                pltpu.VMEM((slabs, rank, cols), jnp.float32),
                pltpu.SemaphoreType.DMA((slabs,)),
                pltpu.SemaphoreType.DMA((width // PIECE,)),
            ],
            compiler_params=pltpu.CompilerParams(vmem_limit_bytes=54 * 2**20),
            cost_estimate=cost(5),
            name=name,
        )(where, snapshot, tests_first, *more)

    def add_up(kernel, name, shape, *args):
        specs = [smem] * (kernel is sum_stack) + [vmem]
        specs += [anywhere] * (len(args) - len(specs))
        return pl.pallas_call(
            kernel,
            out_shape=f32(*shape),
            in_specs=specs,
            out_specs=vmem,
            compiler_params=params,
            cost_estimate=cost(1),
            name=name,
        )(*args)

    rights_first = jnp.transpose(core_right, (1, 0, 2))
    swap = [(0, 1), (1, 0)]
    send = range_part("range_send", flip, 0)
    got = lax.ppermute(send, "zh", swap)

    def reduce(place, snapshot, tests_first, range_sketch, corange_test, core_left, rights_first, send, core_sketch):
        steps = rows // BLOCK

        mine, other = pl.pallas_call(
            products,
            out_shape=(f32(ROWS, 128), f32(ROWS, 128)),
            grid_spec=pltpu.PrefetchScalarGridSpec(
                num_scalar_prefetch=1,
                grid=(steps,),
                in_specs=[
                    pl.BlockSpec((slabs, BLOCK, cols), lambda i, p: (0, i, 0)),
                    pl.BlockSpec((rank, BLOCK), lambda i, p: (0, i)),
                    pl.BlockSpec((size, BLOCK), lambda i, p: (0, i)),
                    anywhere,
                    anywhere,
                ],
                out_specs=[
                    pl.BlockSpec((ROWS, 128), lambda i, p: (0, 0)),
                    pl.BlockSpec((ROWS, 128), lambda i, p: (0, 0)),
                ],
                scratch_shapes=[
                    pltpu.VMEM((LEFT_AT + size, 3 * BLOCK), jnp.bfloat16),
                    pltpu.VMEM((slabs, LEFT_AT + size, cols), jnp.float32),
                    pltpu.VMEM((2, ROWS, 128), jnp.float32),
                    pltpu.VMEM((264, 256), jnp.float32),
                    pltpu.VMEM((8, size), jnp.float32),
                    pltpu.VMEM((slabs, size, cols), jnp.float32),
                    pltpu.SemaphoreType.DMA((slabs,)),
                ],
            ),
            compiler_params=pltpu.CompilerParams(vmem_limit_bytes=60 * 2**20),
            cost_estimate=cost(9),
            name="products",
        )(place, snapshot, corange_test, core_left, rights_first, send)

        part = mine + lax.ppermute(other, "core", swap)
        pieces = lax.all_to_all(part.reshape(16, CHUNK, 128), ("x", "y"), 0, 0, tiled=True)
        copies = add_up(sum_pieces, "sum_pieces", (8, CHUNK, 128), pieces)
        stack = lax.all_to_all(copies, ("zh", "zl"), 0, 0, tiled=True)
        keep = range_part("range_keep", place, 1, range_sketch, copies)
        copies = add_up(sum_stack, "sum_stack", (16, CHUNK, 128), place, stack, keep)
        mine = lax.all_to_all(copies, ("x", "y"), 0, 0, tiled=True).reshape(ROWS, 128)
        other = lax.ppermute(mine, "core", swap)
        corange_out, core_out = pl.pallas_call(
            finish,
            out_shape=(f32(rank, slabs, cols), f32(size, size)),
            in_specs=[smem] + [vmem] * 3,
            out_specs=[vmem] * 2,
            compiler_params=params,
            cost_estimate=cost(2),
            name="finish",
        )(place, mine, other, core_sketch)
        return keep, corange_out, core_out

    def nothing(*_):
        return tuple(jnp.zeros(shape, jnp.float32) for shape in ((rank, width), (rank, slabs, cols), (size, size)))

    keep, corange_out, core_out = lax.cond(
        place[0] >= 0, reduce, nothing,
        place, snapshot, tests_first, range_sketch, corange_test, core_left, rights_first, send, core_sketch,
    )
    range_out = keep + got

    return range_out, jnp.transpose(corange_out, (1, 0, 2)), core_out


def solution(mesh):
    fine = Mesh(mesh.devices.reshape(4, 4, 4, 2, 2), ("zl", "x", "y", "core", "zh"))
    row = ("zl", "x", "y", "core")
    placed = (
        P(None, row, "zh"),
        P(None, None, "zh"),
        P(None, row),
        P(None, row),
        P(None, None, "zh"),
        P(None, row + ("zh",)),
        P(),
    )
    return jax.shard_map(
        on_device,
        mesh=fine,
        in_specs=placed,
        out_specs=(P(None, row + ("zh",)), P(None, None, "zh"), P()),
        check_vma=False,
    )
```

```python
import jax
import jax.numpy as jnp
from jax import lax
from jax.experimental import pallas as pl
from jax.experimental.pallas import tpu as pltpu
from jax.sharding import Mesh
from jax.sharding import PartitionSpec as P

ROWS = 896
CORE_AT = 544
EXTRA_AT = 808
CHUNK = 56
SLAB = 136
LEFT_AT = 144
PIECE = 512
BLOCK = 512


def split(x):
    high = x.astype(jnp.bfloat16)
    low = (x - high.astype(jnp.float32)).astype(jnp.bfloat16)
    return high, low


NT = (((1,), (1,)), ((), ()))


def products(
    place, snap_ref, corange_ref, left_ref, right_hbm, after,
    mine_ref, other_ref,
    tests, acc, pay, core_acc, extra_acc, right, sem,
):
    step = pl.program_id(0)
    steps = pl.num_programs(0)
    slabs, _, cols = snap_ref.shape
    rank = corange_ref.shape[0]
    size = left_ref.shape[0]
    more = size - 256
    loads = [pltpu.make_async_copy(right_hbm.at[:, j, :], right.at[j], sem.at[j]) for j in range(slabs)]

    @pl.when(step == 0)
    def _():
        for copy in loads:
            copy.start()
        acc[...] = jnp.zeros_like(acc)
        tests[rank:LEFT_AT] = jnp.zeros((LEFT_AT - rank, tests.shape[1]), jnp.bfloat16)

    high, low = split(corange_ref[...])
    tests[:rank] = jnp.concatenate([high, high, low], axis=1)
    high, low = split(left_ref[...])
    tests[LEFT_AT:] = jnp.concatenate([high, high, low], axis=1)
    for j in range(slabs):
        high, low = split(snap_ref[j])
        acc[j] += jnp.dot(
            tests[...], jnp.concatenate([high, low, high], axis=0), preferred_element_type=jnp.float32
        )

    @pl.when(step == steps - 1)
    def _():
        lefts, rights = [], []
        for j in range(slabs):
            for half in range(2):
                pay[place[1] ^ half, SLAB * j : SLAB * (j + 1), :] = acc[j, :SLAB, 128 * half : 128 * half + 128]
            loads[j].wait()
            high, low = split(acc[j, LEFT_AT:])
            lefts += [high, high, low]
            high, low = split(right[j])
            rights += [high, low, high]
        left_all = jnp.concatenate(lefts, axis=1)
        right_all = jnp.concatenate(rights, axis=1)
        core_acc[:size] = lax.dot_general(left_all, right_all[:256], NT, preferred_element_type=jnp.float32)
        extra_acc[:more] = lax.dot_general(right_all[256:], left_all, NT, preferred_element_type=jnp.float32)
        for half in range(2):
            lanes = slice(128 * half, 128 * half + 128)
            own = place[1] ^ half
            pay[own, CORE_AT : CORE_AT + size, :] = core_acc[:size, lanes]
            pay[own, EXTRA_AT : EXTRA_AT + more, :] = extra_acc[:more, lanes]
        pay[place[1], EXTRA_AT + 8 : EXTRA_AT + 8 + more, :more] = extra_acc[:more, 256:]
        mine_ref[...] = pay[0]
        other_ref[...] = pay[1]


def range_half(place, snap_hbm, test_hbm, *rest):
    *extra, out_ref, snap, test, test_sem, sem = rest
    kept = extra[0] if len(extra) and extra[0].shape[0] == out_ref.shape[0] and len(extra) == 2 else None
    slabs, width, _ = snap.shape
    count = width // PIECE
    at = place[0] * width
    loads = [pltpu.make_async_copy(test_hbm.at[:, j, :], test.at[j], test_sem.at[j]) for j in range(slabs)]
    for copy in loads:
        copy.start()
    copies = []
    for c in range(count):
        copy = pltpu.make_async_copy(
            snap_hbm.at[:, pl.ds(pl.multiple_of(at + c * PIECE, PIECE), PIECE), :],
            snap.at[:, pl.ds(c * PIECE, PIECE), :],
            sem.at[c],
        )
        copy.start()
        copies.append(copy)
    tests = []
    for j in range(slabs):
        loads[j].wait()
        high, low = split(test[j])
        tests += [high, high, low]
    tests = jnp.concatenate(tests, axis=1)
    for c in range(count):
        copies[c].wait()
        pieces = []
        for j in range(slabs):
            high, low = split(snap[j, c * PIECE : (c + 1) * PIECE, :])
            pieces += [high, low, high]
        cols = slice(c * PIECE, (c + 1) * PIECE)
        part = lax.dot_general(tests, jnp.concatenate(pieces, axis=1), NT, preferred_element_type=jnp.float32)
        out_ref[:, cols] = part if kept is None else kept[:, cols] + part


def sum_pieces(pieces_ref, *rest):
    out_ref = rest[-1]
    total = pieces_ref[0]
    for k in range(1, pieces_ref.shape[0]):
        total += pieces_ref[k]
    for k in range(out_ref.shape[0]):
        out_ref[k] = total


def sum_stack(place, stack_ref, *rest):
    out_ref = rest[-1]
    near = stack_ref[4 * place[0]]
    far = stack_ref[4 - 4 * place[0]]
    for k in range(1, 4):
        near += stack_ref[4 * place[0] + k]
        far += stack_ref[4 - 4 * place[0] + k]
    at = CHUNK * place[2] + lax.broadcasted_iota(jnp.int32, near.shape, 0)
    total = jnp.where(at >= CORE_AT, near + far, near)
    for k in range(out_ref.shape[0]):
        out_ref[k] = total


def turn_out(place, part_ref, corange_ref):
    rank, slabs, _ = corange_ref.shape
    for j in range(slabs):
        corange_ref[:, j, :] = part_ref[SLAB * j : SLAB * j + rank, :]


def finish(place, mine_ref, other_ref, core_sketch_ref, before, corange_ref, core_ref):
    turn_out(place, other_ref, corange_ref)
    size = core_ref.shape[0]
    more = size - 256
    for own in range(2):

        @pl.when(place[1] == own)
        def _():
            for half, part in ((own, mine_ref), (1 - own, other_ref)):
                lanes = slice(128 * half, 128 * half + 128)
                core_ref[:, lanes] = core_sketch_ref[:, lanes] + part[CORE_AT : CORE_AT + size, :]
                block = jnp.concatenate([part[EXTRA_AT : EXTRA_AT + 8, :], jnp.zeros((120, 128), jnp.float32)], axis=0)
                turned = block.T
                core_ref[lanes, 256:] = core_sketch_ref[lanes, 256:] + turned[:, :more]
                if half == 0:
                    block = jnp.concatenate(
                        [part[EXTRA_AT + 8 : EXTRA_AT + 16, :], jnp.zeros((120, 128), jnp.float32)], axis=0
                    )
                    turned = block.T
                    core_ref[256:, 256:] = core_sketch_ref[256:, 256:] + turned[:more, :more]


def on_device(snapshot, range_test, corange_test, core_left, core_right, range_sketch, core_sketch):
    slabs, rows, cols = snapshot.shape
    rank = range_test.shape[1]
    size = core_left.shape[0]
    width = rows // 2
    column = lax.axis_index("zh")
    place = jnp.stack([column, lax.axis_index("core"), lax.axis_index(("x", "y"))]).astype(jnp.int32)
    flip = jnp.stack([1 - column]).astype(jnp.int32)
    vmem = pl.BlockSpec(memory_space=pltpu.VMEM)
    smem = pl.BlockSpec(memory_space=pltpu.SMEM)
    anywhere = pl.BlockSpec(memory_space=pl.ANY)
    params = pltpu.CompilerParams(vmem_limit_bytes=16 * 2**20)
    f32 = lambda *shape: jax.ShapeDtypeStruct(shape, jnp.float32)

    def cost(us):
        return pl.CostEstimate(flops=int(us * 1e9), bytes_accessed=int(us * 3e6), transcendentals=0)

    tests_first = jnp.transpose(range_test, (1, 0, 2))
    def range_part(name, where, kept, *more):
        return pl.pallas_call(
            range_half,
            out_shape=f32(rank, width),
            in_specs=[smem, anywhere, anywhere] + [vmem] * kept + [anywhere] * (len(more) - kept),
            out_specs=vmem,
            scratch_shapes=[
                pltpu.VMEM((slabs, width, cols), jnp.float32),
                pltpu.VMEM((slabs, rank, cols), jnp.float32),
                pltpu.SemaphoreType.DMA((slabs,)),
                pltpu.SemaphoreType.DMA((width // PIECE,)),
            ],
            compiler_params=pltpu.CompilerParams(vmem_limit_bytes=54 * 2**20),
            cost_estimate=cost(5),
            name=name,
        )(where, snapshot, tests_first, *more)

    def add_up(kernel, name, shape, *args):
        specs = [smem] * (kernel is sum_stack) + [vmem]
        specs += [anywhere] * (len(args) - len(specs))
        return pl.pallas_call(
            kernel,
            out_shape=f32(*shape),
            in_specs=specs,
            out_specs=vmem,
            compiler_params=params,
            cost_estimate=cost(1),
            name=name,
        )(*args)

    rights_first = jnp.transpose(core_right, (1, 0, 2))
    swap = [(0, 1), (1, 0)]
    send = range_part("range_send", flip, 0)
    got = lax.ppermute(send, "zh", swap)

    def reduce(place, snapshot, tests_first, range_sketch, corange_test, core_left, rights_first, send, core_sketch):
        steps = rows // BLOCK

        mine, other = pl.pallas_call(
            products,
            out_shape=(f32(ROWS, 128), f32(ROWS, 128)),
            grid_spec=pltpu.PrefetchScalarGridSpec(
                num_scalar_prefetch=1,
                grid=(steps,),
                in_specs=[
                    pl.BlockSpec((slabs, BLOCK, cols), lambda i, p: (0, i, 0)),
                    pl.BlockSpec((rank, BLOCK), lambda i, p: (0, i)),
                    pl.BlockSpec((size, BLOCK), lambda i, p: (0, i)),
                    anywhere,
                    anywhere,
                ],
                out_specs=[
                    pl.BlockSpec((ROWS, 128), lambda i, p: (0, 0)),
                    pl.BlockSpec((ROWS, 128), lambda i, p: (0, 0)),
                ],
                scratch_shapes=[
                    pltpu.VMEM((LEFT_AT + size, 3 * BLOCK), jnp.bfloat16),
                    pltpu.VMEM((slabs, LEFT_AT + size, cols), jnp.float32),
                    pltpu.VMEM((2, ROWS, 128), jnp.float32),
                    pltpu.VMEM((264, 256), jnp.float32),
                    pltpu.VMEM((8, size), jnp.float32),
                    pltpu.VMEM((slabs, size, cols), jnp.float32),
                    pltpu.SemaphoreType.DMA((slabs,)),
                ],
            ),
            compiler_params=pltpu.CompilerParams(vmem_limit_bytes=60 * 2**20),
            cost_estimate=cost(9),
            name="products",
        )(place, snapshot, corange_test, core_left, rights_first, send)

        part = mine + lax.ppermute(other, "core", swap)
        pieces = lax.all_to_all(part.reshape(16, CHUNK, 128), ("x", "y"), 0, 0, tiled=True)
        copies = add_up(sum_pieces, "sum_pieces", (8, CHUNK, 128), pieces)
        stack = lax.all_to_all(copies, ("zh", "zl"), 0, 0, tiled=True)
        keep = range_part("range_keep", place, 1, range_sketch, copies)
        copies = add_up(sum_stack, "sum_stack", (16, CHUNK, 128), place, stack, keep)
        mine = lax.all_to_all(copies, ("x", "y"), 0, 0, tiled=True).reshape(ROWS, 128)
        other = lax.ppermute(mine, "core", swap)
        whole = [pl.BlockSpec((ROWS, 128), lambda i, p: (0, 0))] * 2
        core_spec = pl.BlockSpec((size, size), lambda i, p: (0, 0))
        own_half = pl.pallas_call(
            turn_out,
            out_shape=f32(rank, slabs, cols),
            grid_spec=pltpu.PrefetchScalarGridSpec(
                num_scalar_prefetch=1,
                grid=(1,),
                in_specs=whole[:1],
                out_specs=pl.BlockSpec((rank, slabs, 128), lambda i, p: (0, 0, p[1])),
            ),
            compiler_params=params,
            cost_estimate=cost(1),
            name="own_half",
        )(place, mine)
        corange_out, core_out = pl.pallas_call(
            finish,
            out_shape=(f32(rank, slabs, cols), f32(size, size)),
            grid_spec=pltpu.PrefetchScalarGridSpec(
                num_scalar_prefetch=1,
                grid=(1,),
                in_specs=whole + [core_spec, anywhere],
                out_specs=[pl.BlockSpec((rank, slabs, 128), lambda i, p: (0, 0, 1 - p[1])), core_spec],
            ),
            input_output_aliases={4: 0},
            compiler_params=params,
            cost_estimate=cost(2),
            name="finish",
        )(place, mine, other, core_sketch, own_half)
        return keep, corange_out, core_out

    def nothing(*_):
        return tuple(jnp.zeros(shape, jnp.float32) for shape in ((rank, width), (rank, slabs, cols), (size, size)))

    keep, corange_out, core_out = lax.cond(
        place[0] >= 0, reduce, nothing,
        place, snapshot, tests_first, range_sketch, corange_test, core_left, rights_first, send, core_sketch,
    )
    range_out = keep + got

    return range_out, jnp.transpose(corange_out, (1, 0, 2)), core_out


def solution(mesh):
    fine = Mesh(mesh.devices.reshape(4, 4, 4, 2, 2), ("zl", "x", "y", "core", "zh"))
    row = ("zl", "x", "y", "core")
    placed = (
        P(None, row, "zh"),
        P(None, None, "zh"),
        P(None, row),
        P(None, row),
        P(None, None, "zh"),
        P(None, row + ("zh",)),
        P(),
    )
    return jax.shard_map(
        on_device,
        mesh=fine,
        in_specs=placed,
        out_specs=(P(None, row + ("zh",)), P(None, None, "zh"), P()),
        check_vma=False,
    )
```
